128 devices in a mesh: space: 16 (over z, y_lo, core), tm: 8 (over y_hi, x).
Axes of the slice: x: 4, y: 4 (y_hi: 2, y_lo: 2; y = y_hi * 2 + y_lo), z: 4, core: 2. Of those that a mesh axis runs over, the one named last changes fastest.
Arguments:
- snapshots: bfloat16 [640, 4, 131072], P('tm', None, 'space'), may hold values from -6 to 6
- weights: float32 [131072], P(('space', 'tm')), may hold values from 0.3 to 18, as said below
Outputs:
- modes: bfloat16 [128, 4, 131072], P(None, None, ('space', 'tm'))
- spectra: float32 [128, 8, 8], replicated
The draws below stay inside these ranges and needn't reach their ends.
Inputs may be any that keep to these rules, and one draw needn't show every extreme that they name: Positive quadrature weights.
All inputs are finite; a program needn't handle non-finite values.
Results may differ from the reference program's by a relative error of at most 0.0047.
Values may be sent and summed in bfloat16 or wider, within the bound.
No kernel may reach another device: no remote copies, remote signals or barrier semaphores. Data moves between devices by JAX's collectives and lax.ppermute only.
A program may use at most 128 MiB of HBM per device.

```python
import math
import jax
import jax.numpy as jnp
from jax import lax

V = 4
NFFT = 256
BLOCKS = 4
PTS_DEV = 8192
HOP = 128
FREQS = 128
TIME = 640
NPTS = 131072
N_TM = 8


def draw_weights(key, part):
    key = jax.random.fold_in(key, 11)
    position = jnp.arange(NPTS, dtype=jnp.float32) / max(NPTS - 1, 1)
    base = jnp.exp(jax.random.uniform(key, (NPTS,), jnp.float32, jnp.log(0.3), jnp.log(3.0)))
    rise = 3.0
    return (base * rise ** position).astype(jnp.float32)


def level_of(stream_key, shape, shards, least, top_value):
    def one(dim, blocks):
        draws = jax.random.uniform(jax.random.fold_in(jax.random.fold_in(stream_key, 6), dim), (blocks,), jnp.float32, least / len(shards), top_value / len(shards))
        return jnp.repeat(jnp.exp(draws), shape[dim] // blocks).reshape((-1,) + (1,) * (len(shape) - dim - 1))

    gain = one(*shards[0])
    for cut in shards[1:]:
        gain = gain * one(*cut)
    return gain


def normal_values(rng, dims, scale, reach, cuts=(), kind=jnp.bfloat16):
    result = jax.random.normal(rng, dims, jnp.float32) * scale
    if len(cuts) > 0:
        result = level_of(rng, dims, cuts, -0.22, 0.18) * result
    return jnp.clip(result, min=-reach, max=reach).astype(kind)


def setup_inputs(seed: int = 0) -> dict:
    seeds = jax.random.split(jax.random.key(seed), 3)
    snapshots = normal_values(seeds[0], (TIME, V, NPTS), 1.0, 6.0, ((0, 8), (2, 16)))
    weights = draw_weights(jax.random.fold_in(seeds[2], 71), 0)
    return dict(snapshots=snapshots, weights=weights)


def spectral_table():
    steps = jnp.arange(NFFT, dtype=jnp.int32)
    freq = jnp.arange(FREQS, dtype=jnp.int32)
    phase = (freq[:, None] * steps[None, :] % NFFT).astype(jnp.float32) * (2.0 * math.pi / NFFT)
    window = 0.5 - 0.5 * jnp.cos(steps.astype(jnp.float32) * (2.0 * math.pi / NFFT))
    scale = 1.0 / jnp.sqrt(jnp.sum(window * window))
    return jnp.concatenate([window * jnp.cos(phase), -window * jnp.sin(phase)], 0) * scale

def block_coeffs(series):
    values = series.astype(jnp.float32)
    centered = values - lax.optimization_barrier(jnp.mean(values, axis=0, keepdims=True))
    count = series.shape[1]
    width = series.shape[2]
    flat = centered.reshape(series.shape[0], count * width)
    table = spectral_table()
    pieces = []
    for block in range(BLOCKS):
        segment = flat[block * HOP:block * HOP + NFFT]
        coeff = jnp.dot(table, segment, precision=lax.Precision.HIGHEST)
        pieces.append(coeff.astype(jnp.bfloat16).reshape(2, FREQS, count, width))
    return jnp.stack(pieces, 1)

def gram_terms(coeffs, weights):
    shape = coeffs.shape
    values = coeffs.astype(jnp.float32).reshape(2 * BLOCKS, shape[2], shape[3], shape[4])
    return jnp.einsum('cfvp,dfvp->fcd', values * weights, values, precision=lax.Precision.HIGHEST)

def normalize(gram):
    total = jnp.trace(gram, axis1=1, axis2=2) + 1e-06
    return gram * (2.0 * BLOCKS / total)[:, None, None]

def lead_mode(spectra, coeffs):
    shape = coeffs.shape
    values = coeffs.astype(jnp.float32).reshape(2 * BLOCKS, shape[2], shape[3], shape[4])
    start = jnp.ones((spectra.shape[0], 2 * BLOCKS), jnp.float32)
    first = jnp.einsum('fcd,fd->fc', spectra, start, precision=lax.Precision.HIGHEST)
    second = jnp.einsum('fcd,fd->fc', spectra, first, precision=lax.Precision.HIGHEST)
    mode = jnp.einsum('fc,cfvp->fvp', second, values, precision=lax.Precision.HIGHEST)
    return (mode / math.sqrt(2.0 * BLOCKS)).astype(jnp.bfloat16)

def reference(snapshots, weights):
    width = PTS_DEV // N_TM
    groups = NPTS // width
    grouped = snapshots.reshape(TIME, V, groups, width).transpose(2, 0, 1, 3)
    grouped_weights = weights.reshape(groups, width)
    coeffs = lax.map(block_coeffs, grouped)
    partial_grams = lax.map(lambda pair: gram_terms(pair[0], pair[1]), (coeffs, grouped_weights))
    spectra = normalize(lax.optimization_barrier(jnp.sum(partial_grams, axis=0)))
    modes = lax.map(lambda coeff: lead_mode(spectra, coeff), coeffs)
    modes = modes.transpose(1, 2, 0, 3).reshape(FREQS, V, NPTS)
    return (modes, spectra)
```

```python
import functools
import math

import jax
import jax.numpy as jnp
import ml_dtypes
import numpy as np
from jax import lax
from jax.experimental import pallas as pl
from jax.experimental.pallas import tpu as pltpu
from jax.sharding import PartitionSpec as P

NFFT = 256
BLOCKS = 4
HOP = 128
FREQS = 128
TIME = 640
ROWS = 2 * BLOCKS
GROUP = 32
GROUPS = FREQS // GROUP
AXES = ("space", "tm")
F32 = jnp.float32
BF16 = jnp.bfloat16


def tables():
    steps = np.arange(NFFT)
    phase = (np.arange(FREQS)[:, None] * steps[None, :] % NFFT) * (2.0 * math.pi / NFFT)
    window = 0.5 - 0.5 * np.cos(steps * (2.0 * math.pi / NFFT))
    full = np.concatenate([window * np.cos(phase), -window * np.sin(phase)], 0)
    full = (full / np.sqrt(np.sum(window * window))).astype(np.float32)
    high = full.astype(ml_dtypes.bfloat16)
    low = (full - high.astype(np.float32)).astype(ml_dtypes.bfloat16)
    split = np.concatenate([high, low], 0)
    sums = (high.astype(np.float64) + low.astype(np.float64)).sum(1, keepdims=True)
    return full, split, sums.astype(np.float32)


def pack_kernel(x_ref, out_ref):
    out_ref[0] = jnp.transpose(x_ref[...], (1, 0, 2))


def pack(x, members):
    steps, count, points = x.shape
    width = points // members
    return pl.pallas_call(
        pack_kernel,
        grid=(members,),
        in_specs=[pl.BlockSpec((steps, count, width), lambda i: (0, 0, i))],
        out_specs=pl.BlockSpec((1, count, steps, width), lambda i: (i, 0, 0, 0)),
        out_shape=jax.ShapeDtypeStruct((members, count, steps, width), x.dtype),
        compiler_params=pltpu.CompilerParams(vmem_limit_bytes=32 << 20),
    )(x)


def gram_kernel(x_ref, w_ref, split_ref, sums_ref, gram_ref, mean_ref, coef_ref, acc_ref):
    step = pl.program_id(0)
    count = x_ref.shape[1]
    width = x_ref.shape[3]

    @pl.when(step == 0)
    def _():
        acc_ref[...] = jnp.zeros_like(acc_ref)

    split = split_ref[...]
    sums = sums_ref[...]
    for v in range(count):
        x = x_ref[:, v].reshape(TIME, width)
        mean = jnp.sum(x.astype(F32), axis=0, keepdims=True) * (1.0 / TIME)
        mean_ref[v : v + 1, :] = mean
        shift = sums * mean
        for b in range(BLOCKS):
            both = jnp.dot(split, x[b * HOP : b * HOP + NFFT], preferred_element_type=F32)
            coef = (both[:NFFT] + both[NFFT:] - shift).astype(BF16)
            for r in range(2):
                for g in range(GROUPS):
                    rows = coef[r * FREQS + g * GROUP : r * FREQS + (g + 1) * GROUP]
                    c = r * BLOCKS + b
                    coef_ref[g, c * GROUP : (c + 1) * GROUP, v * width : (v + 1) * width] = rows
    weights = jnp.concatenate([w_ref[...]] * count, axis=1)
    for g in range(GROUPS):
        a = coef_ref[g]
        weighted = (a.astype(F32) * weights).astype(BF16)
        acc_ref[g] += lax.dot_general(
            weighted, a, (((1,), (1,)), ((), ())), preferred_element_type=F32
        )

    @pl.when(step == pl.num_programs(0) - 1)
    def _():
        size = ROWS * GROUP
        row = lax.broadcasted_iota(jnp.int32, (GROUP, size), 0)
        lane = lax.broadcasted_iota(jnp.int32, (GROUP, size), 1)
        same = lane % GROUP == row
        lane1 = lax.broadcasted_iota(jnp.int32, (1, FREQS), 1)
        for g in range(GROUPS):
            last = jnp.zeros((1, FREQS), F32)
            for c in range(ROWS):
                block = acc_ref[g, c * GROUP : (c + 1) * GROUP, :]
                line = jnp.sum(jnp.where(same, block, 0.0), axis=0, keepdims=True)
                if c < BLOCKS:
                    mine = lane1 // GROUP == c
                    last = last + jnp.where(mine, line[:, FREQS:], 0.0)
                turned = pltpu.roll(line, (size - c * GROUP) % size, 1) if c else line
                gram_ref[g * ROWS + c : g * ROWS + c + 1, :] = turned[:, :FREQS]
            gram_ref[GROUPS * ROWS + g : GROUPS * ROWS + g + 1, :] = last
        gram_ref[GROUPS * ROWS + GROUPS :, :] = jnp.zeros((ROWS - GROUPS, FREQS), F32)


def gram_terms(x, weights, split, sums, width):
    members, count, steps, points = x.shape
    out = (GROUPS + 1) * ROWS
    return pl.pallas_call(
        gram_kernel,
        grid=(points // width,),
        in_specs=[
            pl.BlockSpec((members, count, steps, width), lambda i: (0, 0, 0, i)),
            pl.BlockSpec((1, width), lambda i: (0, i)),
            pl.BlockSpec((2 * NFFT, NFFT), lambda i: (0, 0)),
            pl.BlockSpec((NFFT, 1), lambda i: (0, 0)),
        ],
        out_specs=[
            pl.BlockSpec((out, FREQS), lambda i: (0, 0)),
            pl.BlockSpec((count, width), lambda i: (0, i)),
        ],
        out_shape=[
            jax.ShapeDtypeStruct((out, FREQS), F32),
            jax.ShapeDtypeStruct((count, points), F32),
        ],
        scratch_shapes=[
            pltpu.VMEM((GROUPS, ROWS * GROUP, count * width), BF16),
            pltpu.VMEM((GROUPS, ROWS * GROUP, ROWS * GROUP), F32),
        ],
        compiler_params=pltpu.CompilerParams(vmem_limit_bytes=48 << 20),
    )(x, weights.reshape(1, points), split, sums)


def turn(a, by):
    by = by % ROWS
    return a if by == 0 else jnp.concatenate([a[by:], a[:by]], axis=0)


def lanes(a, by):
    by = by % FREQS
    return a if by == 0 else pltpu.roll(a, by, 1)


def full_gram(packed):
    part = lax.broadcasted_iota(jnp.int32, (ROWS, FREQS), 1) // GROUP
    row = lax.broadcasted_iota(jnp.int32, (ROWS, FREQS), 0)
    out = []
    for k in range(BLOCKS):
        total = jnp.zeros((ROWS, FREQS), F32)
        for g in range(GROUPS):
            moved = lanes(packed[g * ROWS : (g + 1) * ROWS], (g - k) * GROUP)
            total = jnp.where(part == g, moved, total)
        out.append(total)
    rest = packed[GROUPS * ROWS :]
    total = jnp.zeros((ROWS, FREQS), F32)
    for delta in range(1 - BLOCKS, BLOCKS):
        moved = lanes(turn(rest, delta), delta * GROUP)
        total = jnp.where((row < BLOCKS) & (part - row == delta), moved, total)
    out.append(total + turn(total, BLOCKS))
    for k in range(BLOCKS + 1, ROWS):
        out.append(turn(out[ROWS - k], k))
    return out


def power_step(spectra, vector):
    return sum(spectra[k] * turn(vector, k) for k in range(ROWS))


def modes_kernel(packed_ref, x_ref, mean_ref, table_ref, modes_ref, spectra_ref, m_ref, sum_ref):
    count = x_ref.shape[1]
    width = x_ref.shape[3]

    @pl.when(pl.program_id(0) == 0)
    def _():
        gram = full_gram(packed_ref[...])
        trace = jnp.sum(gram[0], axis=0, keepdims=True) + 1e-06
        spectra = [k * (2.0 * BLOCKS / trace) for k in gram]
        row = lax.broadcasted_iota(jnp.int32, (ROWS, FREQS), 0)
        for d in range(ROWS):
            total = jnp.zeros((ROWS, FREQS), F32)
            for c in range(ROWS):
                total = jnp.where(row == c, spectra[(d - c) % ROWS], total)
            spectra_ref[d * ROWS : (d + 1) * ROWS, :] = total
        first = power_step(spectra, jnp.ones((ROWS, FREQS), F32))
        lead = power_step(spectra, first) * (1.0 / math.sqrt(2.0 * BLOCKS))
        padded = jnp.concatenate([lead, jnp.zeros((FREQS - ROWS, FREQS), F32)], axis=0)
        lead = padded.T
        total = [jnp.zeros((FREQS, HOP), F32) for _ in range(BLOCKS + 1)]
        for b in range(BLOCKS):
            for r in range(2):
                c = r * BLOCKS + b
                part = lead[:, c : c + 1] * table_ref[r * FREQS : (r + 1) * FREQS, :]
                total[b] = total[b] + part[:, :HOP]
                total[b + 1] = total[b + 1] + part[:, HOP:]
        total = jnp.concatenate(total, axis=1)
        high = total.astype(BF16)
        low = (total - high.astype(F32)).astype(BF16)
        m_ref[:FREQS] = high
        m_ref[FREQS:] = low
        sum_ref[...] = jnp.sum(high.astype(F32) + low.astype(F32), axis=1, keepdims=True)

    out = []
    for v in range(count):
        x = x_ref[:, v].reshape(TIME, width)
        both = jnp.dot(m_ref[...], x, preferred_element_type=F32)
        mode = both[:FREQS] + both[FREQS:] - sum_ref[...] * mean_ref[v : v + 1, :]
        out.append(mode.astype(BF16))
    modes_ref[...] = pltpu.einshape("vfp->fvp", jnp.stack(out, 0))


def modes_of(packed, x, mean, table, width):
    members, count, steps, points = x.shape
    return pl.pallas_call(
        modes_kernel,
        grid=(points // width,),
        in_specs=[
            pl.BlockSpec(packed.shape, lambda i: (0, 0)),
            pl.BlockSpec((members, count, steps, width), lambda i: (0, 0, 0, i)),
            pl.BlockSpec((count, width), lambda i: (0, i)),
            pl.BlockSpec((NFFT, NFFT), lambda i: (0, 0)),
        ],
        out_specs=[
            pl.BlockSpec((FREQS, count, width), lambda i: (0, 0, i)),
            pl.BlockSpec((ROWS * ROWS, FREQS), lambda i: (0, 0)),
        ],
        out_shape=[
            jax.ShapeDtypeStruct((FREQS, count, points), BF16),
            jax.ShapeDtypeStruct((ROWS * ROWS, FREQS), F32),
        ],
        scratch_shapes=[
            pltpu.VMEM((2 * FREQS, TIME), BF16),
            pltpu.VMEM((FREQS, 1), F32),
        ],
        compiler_params=pltpu.CompilerParams(vmem_limit_bytes=48 << 20),
    )(packed, x, mean, table)


def sum_over_devices(value, devices):
    step = 1
    while step < devices:
        pairs = [(i, i ^ step) for i in range(devices)]
        value = value + lax.ppermute(value, AXES, pairs)
        step *= 2
    return value


def per_device(members, devices, snapshots, weights):
    table, split, sums = tables()
    packed = pack(snapshots, members)
    series = lax.all_to_all(packed, "tm", split_axis=0, concat_axis=0, tiled=True)
    terms, mean = gram_terms(series, weights, jnp.asarray(split), jnp.asarray(sums), 256)
    gram = sum_over_devices(terms, devices)
    modes, spectra = modes_of(gram, series, mean, jnp.asarray(table), 256)
    spectra = spectra.T.reshape(FREQS, ROWS, ROWS)
    return (modes, spectra)


def solution(mesh):
    members = mesh.shape["tm"]
    devices = members * mesh.shape["space"]
    in_specs = (P("tm", None, "space"), P(AXES))
    out_specs = (P(None, None, AXES), P())
    return jax.shard_map(
        functools.partial(per_device, members, devices),
        mesh=mesh,
        in_specs=in_specs,
        out_specs=out_specs,
        check_vma=False,
    )
```

```python
import functools
import math

import jax
import jax.numpy as jnp
import ml_dtypes
import numpy as np
from jax import lax
from jax.experimental import pallas as pl
from jax.experimental.pallas import tpu as pltpu
from jax.sharding import PartitionSpec as P

NFFT = 256
BLOCKS = 4
HOP = 128
FREQS = 128
TIME = 640
ROWS = 2 * BLOCKS
GROUP = 32
GROUPS = FREQS // GROUP
AXES = ("space", "tm")
TILE = 256
ACROSS = 4
PACKS = (2, 8)
PACK_VMEM = 54 << 20
GRAM_VMEM = 24 << 20
STEPS = ((1, 1), (0, 3), (1, 0), (0, 2), (1, 2), (0, 1), (1, 3), (0, 0))
F32 = jnp.float32
BF16 = jnp.bfloat16


def tables():
    steps = np.arange(NFFT)
    phase = (np.arange(FREQS)[:, None] * steps[None, :] % NFFT) * (2.0 * math.pi / NFFT)
    window = 0.5 - 0.5 * np.cos(steps * (2.0 * math.pi / NFFT))
    full = np.concatenate([window * np.cos(phase), -window * np.sin(phase)], 0)
    full = (full / np.sqrt(np.sum(window * window))).astype(np.float32)
    high = full.astype(ml_dtypes.bfloat16)
    low = (full - high.astype(np.float32)).astype(ml_dtypes.bfloat16)
    split = np.concatenate([high, low], 0)
    sums = (high.astype(np.float64) + low.astype(np.float64)).sum(1, keepdims=True)
    return full, split, sums.astype(np.float32)


def shifted(index, step):
    half, across = index >> 2, index & 3
    return ((half + step[0]) & 1) * ACROSS + ((across + step[1]) & 3)


def pack_kernel(steps, x_ref, *refs):
    out_refs, (held_ref, sem_ref) = refs[:-2], refs[-2:]
    me = lax.axis_index("tm")
    width = held_ref.shape[3]
    copies = []
    for k, step in enumerate(steps):
        lane = pl.multiple_of(shifted(me, step) * width, width)
        copy = pltpu.make_async_copy(
            x_ref.at[:, :, pl.ds(lane, width)], held_ref.at[k], sem_ref.at[k]
        )
        copy.start()
        copies.append(copy)
    for k in range(len(steps)):
        copies[k].wait()
        for at in range(0, width, TILE):
            piece = held_ref[k, :, :, at : at + TILE]
            out_refs[k][:, :, at : at + TILE] = jnp.transpose(piece, (1, 0, 2))


def pack(x, steps):
    times, count, points = x.shape
    width = points // len(STEPS)
    return pl.pallas_call(
        functools.partial(pack_kernel, steps),
        in_specs=[pl.BlockSpec(memory_space=pl.ANY)],
        out_specs=[pl.BlockSpec(memory_space=pltpu.VMEM)] * len(steps),
        out_shape=[jax.ShapeDtypeStruct((count, times, width), x.dtype)] * len(steps),
        scratch_shapes=[
            pltpu.VMEM((len(steps), times, count, width), x.dtype),
            pltpu.SemaphoreType.DMA((len(steps),)),
        ],
        compiler_params=pltpu.CompilerParams(vmem_limit_bytes=PACK_VMEM),
    )(x)


def gram_kernel(*refs):
    members = len(STEPS)
    me = lax.axis_index("tm")
    pieces = refs[:members]
    w_ref, split_ref, sums_ref = refs[members : members + 3]
    gram_ref, x_ref, mean_ref, coef_ref, acc_ref = refs[-5:]
    step = pl.program_id(0)
    count, steps, width = pieces[0].shape

    @pl.when(step == 0)
    def _():
        acc_ref[...] = jnp.zeros_like(acc_ref)

    for k in range(members):
        source = shifted(me, (-STEPS[k][0], -STEPS[k][1]))
        at = pl.multiple_of(source * steps, 16)
        for v in range(count):
            x_ref[v, pl.ds(at, steps), :] = pieces[k][v]

    split = split_ref[...]
    sums = sums_ref[...]
    for v in range(count):
        x = x_ref[v]
        mean = jnp.sum(x.astype(F32), axis=0, keepdims=True) * (1.0 / TIME)
        mean_ref[v : v + 1, :] = mean
        shift = sums * mean
        for b in range(BLOCKS):
            both = jnp.dot(split, x[b * HOP : b * HOP + NFFT], preferred_element_type=F32)
            coef = (both[:NFFT] + both[NFFT:] - shift).astype(BF16)
            for r in range(2):
                for g in range(GROUPS):
                    rows = coef[r * FREQS + g * GROUP : r * FREQS + (g + 1) * GROUP]
                    c = r * BLOCKS + b
                    coef_ref[g, c * GROUP : (c + 1) * GROUP, v * width : (v + 1) * width] = rows
    weights = jnp.concatenate([w_ref[...]] * count, axis=1)
    for g in range(GROUPS):
        a = coef_ref[g]
        weighted = (a.astype(F32) * weights).astype(BF16)
        acc_ref[g] += lax.dot_general(
            weighted, a, (((1,), (1,)), ((), ())), preferred_element_type=F32
        )

    @pl.when(step == pl.num_programs(0) - 1)
    def _():
        size = ROWS * GROUP
        row = lax.broadcasted_iota(jnp.int32, (GROUP, size), 0)
        lane = lax.broadcasted_iota(jnp.int32, (GROUP, size), 1)
        same = lane % GROUP == row
        lane1 = lax.broadcasted_iota(jnp.int32, (1, FREQS), 1)
        for g in range(GROUPS):
            last = jnp.zeros((1, FREQS), F32)
            for c in range(ROWS):
                block = acc_ref[g, c * GROUP : (c + 1) * GROUP, :]
                line = jnp.sum(jnp.where(same, block, 0.0), axis=0, keepdims=True)
                if c < BLOCKS:
                    mine = lane1 // GROUP == c
                    last = last + jnp.where(mine, line[:, FREQS:], 0.0)
                turned = pltpu.roll(line, (size - c * GROUP) % size, 1) if c else line
                at = g * ROWS + c
                gram_ref[at : at + 1, :] = turned[:, :FREQS]
            at = GROUPS * ROWS + g
            gram_ref[at : at + 1, :] = last
        gram_ref[GROUPS * ROWS + GROUPS :, :] = jnp.zeros((ROWS - GROUPS, FREQS), F32)


def gram_terms(pieces, weights, split, sums):
    count, steps, points = pieces[0].shape
    out = (GROUPS + 1) * ROWS
    piece = pl.BlockSpec((count, steps, TILE), lambda i: (0, 0, i))
    return pl.pallas_call(
        gram_kernel,
        grid=(points // TILE,),
        in_specs=[piece] * len(pieces)
        + [
            pl.BlockSpec((1, TILE), lambda i: (0, i)),
            pl.BlockSpec(split.shape, lambda i: (0, 0)),
            pl.BlockSpec(sums.shape, lambda i: (0, 0)),
        ],
        out_specs=[
            pl.BlockSpec((out, FREQS), lambda i: (0, 0)),
            pl.BlockSpec((count, TIME, TILE), lambda i: (0, 0, i)),
            pl.BlockSpec((count, TILE), lambda i: (0, i)),
        ],
        out_shape=[
            jax.ShapeDtypeStruct((out, FREQS), F32),
            jax.ShapeDtypeStruct((count, TIME, points), BF16),
            jax.ShapeDtypeStruct((count, points), F32),
        ],
        scratch_shapes=[
            pltpu.VMEM((GROUPS, ROWS * GROUP, count * TILE), BF16),
            pltpu.VMEM((GROUPS, ROWS * GROUP, ROWS * GROUP), F32),
        ],
        compiler_params=pltpu.CompilerParams(vmem_limit_bytes=GRAM_VMEM),
    )(*pieces, weights.reshape(1, -1), split, sums)


def turn(a, by):
    by = by % ROWS
    return a if by == 0 else jnp.concatenate([a[by:], a[:by]], axis=0)


def lanes(a, by):
    by = by % FREQS
    return a if by == 0 else pltpu.roll(a, by, 1)


def full_gram(packed):
    part = lax.broadcasted_iota(jnp.int32, (ROWS, FREQS), 1) // GROUP
    row = lax.broadcasted_iota(jnp.int32, (ROWS, FREQS), 0)
    out = []
    for k in range(BLOCKS):
        total = jnp.zeros((ROWS, FREQS), F32)
        for g in range(GROUPS):
            moved = lanes(packed[g * ROWS : (g + 1) * ROWS], (g - k) * GROUP)
            total = jnp.where(part == g, moved, total)
        out.append(total)
    rest = packed[GROUPS * ROWS :]
    total = jnp.zeros((ROWS, FREQS), F32)
    for delta in range(1 - BLOCKS, BLOCKS):
        moved = lanes(turn(rest, delta), delta * GROUP)
        total = jnp.where((row < BLOCKS) & (part - row == delta), moved, total)
    out.append(total + turn(total, BLOCKS))
    for k in range(BLOCKS + 1, ROWS):
        out.append(turn(out[ROWS - k], k))
    return out


def power_step(spectra, vector):
    return sum(spectra[k] * turn(vector, k) for k in range(ROWS))


def modes_kernel(packed_ref, x_ref, mean_ref, table_ref, modes_ref, spectra_ref, m_ref, sum_ref):
    count, _, width = x_ref.shape

    @pl.when(pl.program_id(0) == 0)
    def _():
        gram = full_gram(packed_ref[...])
        trace = jnp.sum(gram[0], axis=0, keepdims=True) + 1e-06
        spectra = [k * (2.0 * BLOCKS / trace) for k in gram]
        row = lax.broadcasted_iota(jnp.int32, (ROWS, FREQS), 0)
        for d in range(ROWS):
            total = jnp.zeros((ROWS, FREQS), F32)
            for c in range(ROWS):
                total = jnp.where(row == c, spectra[(d - c) % ROWS], total)
            spectra_ref[d * ROWS : (d + 1) * ROWS, :] = total
        first = power_step(spectra, jnp.ones((ROWS, FREQS), F32))
        lead = power_step(spectra, first) * (1.0 / math.sqrt(2.0 * BLOCKS))
        padded = jnp.concatenate([lead, jnp.zeros((FREQS - ROWS, FREQS), F32)], axis=0)
        lead = padded.T
        total = [jnp.zeros((FREQS, HOP), F32) for _ in range(BLOCKS + 1)]
        for b in range(BLOCKS):
            for r in range(2):
                c = r * BLOCKS + b
                part = lead[:, c : c + 1] * table_ref[r * FREQS : (r + 1) * FREQS, :]
                total[b] = total[b] + part[:, :HOP]
                total[b + 1] = total[b + 1] + part[:, HOP:]
        total = jnp.concatenate(total, axis=1)
        high = total.astype(BF16)
        low = (total - high.astype(F32)).astype(BF16)
        m_ref[:FREQS] = high
        m_ref[FREQS:] = low
        sum_ref[...] = jnp.sum(high.astype(F32) + low.astype(F32), axis=1, keepdims=True)

    out = []
    for v in range(count):
        x = x_ref[v]
        both = jnp.dot(m_ref[...], x, preferred_element_type=F32)
        mode = both[:FREQS] + both[FREQS:] - sum_ref[...] * mean_ref[v : v + 1, :]
        out.append(mode.astype(BF16))
    modes_ref[...] = pltpu.einshape("vfp->fvp", jnp.stack(out, 0))


def modes_of(packed, x, mean, table, width):
    count, _, points = x.shape
    return pl.pallas_call(
        modes_kernel,
        grid=(points // width,),
        in_specs=[
            pl.BlockSpec(packed.shape, lambda i: (0, 0)),
            pl.BlockSpec((count, TIME, width), lambda i: (0, 0, i)),
            pl.BlockSpec((count, width), lambda i: (0, i)),
            pl.BlockSpec((NFFT, NFFT), lambda i: (0, 0)),
        ],
        out_specs=[
            pl.BlockSpec((FREQS, count, width), lambda i: (0, 0, i)),
            pl.BlockSpec((ROWS * ROWS, FREQS), lambda i: (0, 0)),
        ],
        out_shape=[
            jax.ShapeDtypeStruct((FREQS, count, points), BF16),
            jax.ShapeDtypeStruct((ROWS * ROWS, FREQS), F32),
        ],
        scratch_shapes=[
            pltpu.VMEM((2 * FREQS, TIME), BF16),
            pltpu.VMEM((FREQS, 1), F32),
        ],
        compiler_params=pltpu.CompilerParams(vmem_limit_bytes=48 << 20),
    )(packed, x, mean, table)


def place(space, tm):
    z, low, core = space // 4, space // 2 % 2, space % 2
    return z, tm // ACROSS * 2 + low, tm % ACROSS, core


def device_at(z, y, x, core):
    return (z * 4 + y % 2 * 2 + core) * 8 + y // 2 * ACROSS + x


def sum_over_devices(value):
    for flip in ((0, 0, 0, 1), (0, 0, 1, 0), (0, 0, 3, 0), (0, 1, 0, 0), (0, 3, 0, 0), (1, 0, 0, 0), (3, 0, 0, 0)):
        pairs = []
        for i in range(128):
            here = place(i // 8, i % 8)
            pairs.append((i, device_at(*(a ^ b for a, b in zip(here, flip)))))
        value = value + lax.ppermute(value, AXES, pairs)
    return value


def per_device(members, devices, snapshots, weights):
    table, split, sums = tables()
    split, sums = jnp.asarray(split), jnp.asarray(sums)
    pieces = []
    for first, end in zip((0,) + PACKS[:-1], PACKS):
        for step, piece in zip(STEPS[first:end], pack(snapshots, STEPS[first:end])):
            if step != (0, 0):
                pairs = [(m, shifted(m, step)) for m in range(members)]
                piece = lax.ppermute(piece, "tm", pairs)
            pieces.append(piece)
    gram, series, mean = gram_terms(pieces, weights, split, sums)
    gram = sum_over_devices(gram)
    modes, spectra = modes_of(gram, series, mean, jnp.asarray(table), TILE)
    spectra = spectra.T.reshape(FREQS, ROWS, ROWS)
    return (modes, spectra)


def solution(mesh):
    members = mesh.shape["tm"]
    devices = members * mesh.shape["space"]
    in_specs = (P("tm", None, "space"), P(AXES))
    out_specs = (P(None, None, AXES), P())
    return jax.shard_map(
        functools.partial(per_device, members, devices),
        mesh=mesh,
        in_specs=in_specs,
        out_specs=out_specs,
        check_vma=False,
    )
```

```python
import functools
import math

import jax
import jax.numpy as jnp
import ml_dtypes
import numpy as np
from jax import lax
from jax.experimental import pallas as pl
from jax.experimental.pallas import tpu as pltpu
from jax.sharding import PartitionSpec as P

NFFT = 256
BLOCKS = 4
HOP = 128
FREQS = 128
TIME = 640
ROWS = 2 * BLOCKS
GROUP = 32
GROUPS = FREQS // GROUP
AXES = ("space", "tm")
TILE = 256
WIDE = 512
ACROSS = 4
PACKS = (2, 7, 8)
WHOLE = 7
DEPTH = 5
PACK_VMEM = 54 << 20
GRAM_VMEM = 24 << 20
STEPS = ((1, 1), (0, 3), (1, 0), (0, 2), (1, 2), (0, 1), (1, 3), (0, 0))
F32 = jnp.float32
BF16 = jnp.bfloat16


def tables():
    steps = np.arange(NFFT)
    phase = (np.arange(FREQS)[:, None] * steps[None, :] % NFFT) * (2.0 * math.pi / NFFT)
    window = 0.5 - 0.5 * np.cos(steps * (2.0 * math.pi / NFFT))
    full = np.concatenate([window * np.cos(phase), -window * np.sin(phase)], 0)
    full = (full / np.sqrt(np.sum(window * window))).astype(np.float32)
    high = full.astype(ml_dtypes.bfloat16)
    low = (full - high.astype(np.float32)).astype(ml_dtypes.bfloat16)
    split = np.concatenate([high, low], 0)
    sums = (high.astype(np.float64) + low.astype(np.float64)).sum(1, keepdims=True)
    return full, split, sums.astype(np.float32)


def shifted(index, step):
    half, across = index >> 2, index & 3
    return ((half + step[0]) & 1) * ACROSS + ((across + step[1]) & 3)


def parts_of(k):
    return 2 if WHOLE <= k < len(STEPS) - 1 else 1


def pack_kernel(first, end, x_ref, *refs):
    out_refs, (held_ref, sem_ref) = list(refs[:-2]), refs[-2:]
    me = lax.axis_index("tm")
    width = held_ref.shape[3]
    copies = []
    for k in range(first, end):
        lane = pl.multiple_of(shifted(me, STEPS[k]) * width, width)
        copy = pltpu.make_async_copy(
            x_ref.at[:, :, pl.ds(lane, width)], held_ref.at[k - first], sem_ref.at[k - first]
        )
        copy.start()
        copies.append(copy)
    for k in range(first, end):
        copies[k - first].wait()
        size = width // parts_of(k)
        for start in range(0, width, size):
            out_ref = out_refs.pop(0)
            for at in range(0, size, TILE):
                piece = held_ref[k - first, :, :, start + at : start + at + TILE]
                out_ref[:, :, at : at + TILE] = jnp.transpose(piece, (1, 0, 2))


def pack(x, first, end):
    times, count, points = x.shape
    width = points // len(STEPS)
    sizes = [width // parts_of(k) for k in range(first, end) for _ in range(parts_of(k))]
    out = pl.pallas_call(
        functools.partial(pack_kernel, first, end),
        in_specs=[pl.BlockSpec(memory_space=pl.ANY)],
        out_specs=[pl.BlockSpec(memory_space=pltpu.VMEM)] * len(sizes),
        out_shape=[jax.ShapeDtypeStruct((count, times, size), x.dtype) for size in sizes],
        scratch_shapes=[
            pltpu.VMEM((end - first, times, count, width), x.dtype),
            pltpu.SemaphoreType.DMA((end - first,)),
        ],
        compiler_params=pltpu.CompilerParams(
            vmem_limit_bytes=PACK_VMEM if first < len(STEPS) - 1 else GRAM_VMEM
        ),
    )(x)
    out = list(out)
    return [[out.pop(0) for _ in range(parts_of(k))] for k in range(first, end)]


def gram_kernel(start, *refs):
    members = len(STEPS)
    pieces = refs[:members]
    w_ref, split_ref, sums_ref, before_ref = refs[members : members + 4]
    gram_ref, x_ref, mean_ref, coef_ref, acc_ref = refs[members + 4 :]
    me = lax.axis_index("tm")
    count, _, points = x_ref.shape
    steps = pieces[0].shape[1]
    rows = []
    for step in STEPS:
        source = shifted(me, (-step[0], -step[1]))
        rows.append(pl.multiple_of(source * steps, 16))
    acc_ref[...] = jnp.zeros_like(acc_ref)

    for tile in range(points // WIDE):
        here = pl.ds(tile * WIDE, WIDE)
        for k in range(members):
            for v in range(count):
                skip = start if pieces[k].shape[2] > points else 0
                there = pl.ds(skip + tile * WIDE, WIDE)
                x_ref[v, pl.ds(rows[k], steps), here] = pieces[k][v, :, there]
        split = split_ref[...]
        sums = sums_ref[...]
        for v in range(count):
            x = x_ref[v, :, here]
            mean = jnp.sum(x.astype(F32), axis=0, keepdims=True) * (1.0 / TIME)
            mean_ref[v : v + 1, here] = mean
            shift = sums * mean
            for b in range(BLOCKS):
                both = jnp.dot(split, x[b * HOP : b * HOP + NFFT], preferred_element_type=F32)
                coef = (both[:NFFT] + both[NFFT:] - shift).astype(BF16)
                for r in range(2):
                    for g in range(GROUPS):
                        part = coef[r * FREQS + g * GROUP : r * FREQS + (g + 1) * GROUP]
                        c = r * BLOCKS + b
                        coef_ref[g, c * GROUP : (c + 1) * GROUP, v * WIDE : (v + 1) * WIDE] = part
        weights = jnp.concatenate([w_ref[:, pl.ds(start + tile * WIDE, WIDE)]] * count, axis=1)
        for g in range(GROUPS):
            a = coef_ref[g]
            weighted = (a.astype(F32) * weights).astype(BF16)
            acc_ref[g] += lax.dot_general(
                weighted, a, (((1,), (1,)), ((), ())), preferred_element_type=F32
            )

    size = ROWS * GROUP
    row = lax.broadcasted_iota(jnp.int32, (GROUP, size), 0)
    lane = lax.broadcasted_iota(jnp.int32, (GROUP, size), 1)
    same = lane % GROUP == row
    lane1 = lax.broadcasted_iota(jnp.int32, (1, FREQS), 1)
    for g in range(GROUPS):
        last = jnp.zeros((1, FREQS), F32)
        for c in range(ROWS):
            block = acc_ref[g, c * GROUP : (c + 1) * GROUP, :]
            line = jnp.sum(jnp.where(same, block, 0.0), axis=0, keepdims=True)
            if c < BLOCKS:
                mine = lane1 // GROUP == c
                last = last + jnp.where(mine, line[:, FREQS:], 0.0)
            turned = pltpu.roll(line, (size - c * GROUP) % size, 1) if c else line
            at = g * ROWS + c
            gram_ref[at : at + 1, :] = before_ref[at : at + 1, :] + turned[:, :FREQS]
        at = GROUPS * ROWS + g
        gram_ref[at : at + 1, :] = before_ref[at : at + 1, :] + last
    gram_ref[GROUPS * ROWS + GROUPS :, :] = jnp.zeros((ROWS - GROUPS, FREQS), F32)


def gram_terms(pieces, weights, split, sums, before, start, points):
    count = pieces[0].shape[0]
    whole = pl.BlockSpec(memory_space=pltpu.VMEM)
    return pl.pallas_call(
        functools.partial(gram_kernel, start),
        in_specs=[whole] * (len(pieces) + 4),
        out_specs=[whole] * 3,
        out_shape=[
            jax.ShapeDtypeStruct(before.shape, F32),
            jax.ShapeDtypeStruct((count, TIME, points), BF16),
            jax.ShapeDtypeStruct((count, points), F32),
        ],
        scratch_shapes=[
            pltpu.VMEM((GROUPS, ROWS * GROUP, count * WIDE), BF16),
            pltpu.VMEM((GROUPS, ROWS * GROUP, ROWS * GROUP), F32),
        ],
        compiler_params=pltpu.CompilerParams(vmem_limit_bytes=GRAM_VMEM),
        cost_estimate=pl.CostEstimate(
            flops=4 * points * count * (2 * NFFT * NFFT * BLOCKS + ROWS * ROWS * GROUP * FREQS),
            bytes_accessed=4 * count * TIME * points,
            transcendentals=0,
        ),
    )(*pieces, weights.reshape(1, -1), split, sums, before)


def turn(a, by):
    by = by % ROWS
    return a if by == 0 else jnp.concatenate([a[by:], a[:by]], axis=0)


def lanes(a, by):
    by = by % FREQS
    return a if by == 0 else pltpu.roll(a, by, 1)


def full_gram(packed):
    part = lax.broadcasted_iota(jnp.int32, (ROWS, FREQS), 1) // GROUP
    row = lax.broadcasted_iota(jnp.int32, (ROWS, FREQS), 0)
    out = []
    for k in range(BLOCKS):
        total = jnp.zeros((ROWS, FREQS), F32)
        for g in range(GROUPS):
            moved = lanes(packed[g * ROWS : (g + 1) * ROWS], (g - k) * GROUP)
            total = jnp.where(part == g, moved, total)
        out.append(total)
    rest = packed[GROUPS * ROWS :]
    total = jnp.zeros((ROWS, FREQS), F32)
    for delta in range(1 - BLOCKS, BLOCKS):
        moved = lanes(turn(rest, delta), delta * GROUP)
        total = jnp.where((row < BLOCKS) & (part - row == delta), moved, total)
    out.append(total + turn(total, BLOCKS))
    for k in range(BLOCKS + 1, ROWS):
        out.append(turn(out[ROWS - k], k))
    return out


def power_step(spectra, vector):
    return sum(spectra[k] * turn(vector, k) for k in range(ROWS))


def modes_kernel(packed_ref, table_ref, *refs):
    x_refs, mean_refs = refs[:2], refs[2:4]
    modes_ref, spectra_ref, m_ref, sum_ref, out_ref, sem_ref = refs[4:]
    count, _, half = x_refs[0].shape
    gram = full_gram(packed_ref[...])
    trace = jnp.sum(gram[0], axis=0, keepdims=True) + 1e-06
    spectra = [k * (2.0 * BLOCKS / trace) for k in gram]
    row = lax.broadcasted_iota(jnp.int32, (ROWS, FREQS), 0)
    for d in range(ROWS):
        total = jnp.zeros((ROWS, FREQS), F32)
        for c in range(ROWS):
            total = jnp.where(row == c, spectra[(d - c) % ROWS], total)
        spectra_ref[d * ROWS : (d + 1) * ROWS, :] = total
    first = power_step(spectra, jnp.ones((ROWS, FREQS), F32))
    lead = power_step(spectra, first) * (1.0 / math.sqrt(2.0 * BLOCKS))
    padded = jnp.concatenate([lead, jnp.zeros((FREQS - ROWS, FREQS), F32)], axis=0)
    lead = padded.T
    total = [jnp.zeros((FREQS, HOP), F32) for _ in range(BLOCKS + 1)]
    for b in range(BLOCKS):
        for r in range(2):
            c = r * BLOCKS + b
            part = lead[:, c : c + 1] * table_ref[r * FREQS : (r + 1) * FREQS, :]
            total[b] = total[b] + part[:, :HOP]
            total[b + 1] = total[b + 1] + part[:, HOP:]
    total = jnp.concatenate(total, axis=1)
    high = total.astype(BF16)
    low = (total - high.astype(F32)).astype(BF16)
    m_ref[:FREQS] = high
    m_ref[FREQS:] = low
    sum_ref[...] = jnp.sum(high.astype(F32) + low.astype(F32), axis=1, keepdims=True)

    copies = []
    for tile in range(2 * half // WIDE):
        part, at = divmod(tile * WIDE, half)
        out = []
        for v in range(count):
            x = x_refs[part][v, :, at : at + WIDE]
            both = jnp.dot(m_ref[...], x, preferred_element_type=F32)
            shift = sum_ref[...] * mean_refs[part][v : v + 1, at : at + WIDE]
            out.append((both[:FREQS] + both[FREQS:] - shift).astype(BF16))
        out_ref[tile] = pltpu.einshape("vfp->fvp", jnp.stack(out, 0))
        copy = pltpu.make_async_copy(
            out_ref.at[tile], modes_ref.at[:, :, pl.ds(tile * WIDE, WIDE)], sem_ref.at[tile]
        )
        copy.start()
        copies.append(copy)
    for copy in copies:
        copy.wait()


def modes_of(packed, table, series, means):
    count, _, half = series[0].shape
    whole = pl.BlockSpec(memory_space=pltpu.VMEM)
    tiles = 2 * half // WIDE
    return pl.pallas_call(
        modes_kernel,
        in_specs=[whole] * 6,
        out_specs=[pl.BlockSpec(memory_space=pl.ANY), whole],
        out_shape=[
            jax.ShapeDtypeStruct((FREQS, count, 2 * half), BF16),
            jax.ShapeDtypeStruct((ROWS * ROWS, FREQS), F32),
        ],
        scratch_shapes=[
            pltpu.VMEM((2 * FREQS, TIME), BF16),
            pltpu.VMEM((FREQS, 1), F32),
            pltpu.VMEM((tiles, FREQS, count, WIDE), BF16),
            pltpu.SemaphoreType.DMA((tiles,)),
        ],
        compiler_params=pltpu.CompilerParams(vmem_limit_bytes=GRAM_VMEM),
    )(packed, table, *series, *means)


def place(space, tm):
    z, low, core = space // 4, space // 2 % 2, space % 2
    return z, tm // ACROSS * 2 + low, tm % ACROSS, core


def device_at(z, y, x, core):
    return (z * 4 + y % 2 * 2 + core) * 8 + y // 2 * ACROSS + x


def sum_over_devices(value):
    rounds = [[(0, 0, 0, 1)]]
    rounds += [[tuple(k * (a == axis) for a in range(4)) for k in (1, 2, 3)] for axis in (2, 1, 0)]
    for flips in rounds:
        total = value
        for flip in flips:
            pairs = []
            for i in range(128):
                here = place(i // 8, i % 8)
                pairs.append((i, device_at(*(a ^ b for a, b in zip(here, flip)))))
            total = total + lax.ppermute(value, AXES, pairs)
        value = total
    return value


def per_device(members, devices, snapshots, weights):
    table, split, sums = tables()
    split, sums = jnp.asarray(split), jnp.asarray(sums)
    pieces = []
    for first, end in zip((0,) + PACKS[:-1], PACKS):
        pieces += pack(snapshots, first, end)
    sent = []
    for part in range(2):
        for k, step in enumerate(STEPS[:-1]):
            if part < parts_of(k):
                piece = pieces[k][part]
                if len(sent) >= DEPTH:
                    piece = lax.optimization_barrier((piece, sent[-DEPTH]))[0]
                pairs = [(m, shifted(m, step)) for m in range(members)]
                pieces[k][part] = lax.ppermute(piece, "tm", pairs)
                sent.append(pieces[k][part])
    half = weights.shape[0] // 2
    gram = jnp.zeros(((GROUPS + 1) * ROWS, FREQS), F32)
    series, means = [], []
    for part in range(2):
        mine = [piece[part % len(piece)] for piece in pieces]
        gram, x, mean = gram_terms(mine, weights, split, sums, gram, part * half, half)
        series.append(x)
        means.append(mean)
    gram = sum_over_devices(gram)
    modes, spectra = modes_of(gram, jnp.asarray(table), series, means)
    spectra = spectra.T.reshape(FREQS, ROWS, ROWS)
    return (modes, spectra)


def solution(mesh):
    members = mesh.shape["tm"]
    devices = members * mesh.shape["space"]
    in_specs = (P("tm", None, "space"), P(AXES))
    out_specs = (P(None, None, AXES), P())
    return jax.shard_map(
        functools.partial(per_device, members, devices),
        mesh=mesh,
        in_specs=in_specs,
        out_specs=out_specs,
        check_vma=False,
    )
```

```python
import functools
import math

import jax
import jax.numpy as jnp
import ml_dtypes
import numpy as np
from jax import lax
from jax.experimental import pallas as pl
from jax.experimental.pallas import tpu as pltpu
from jax.sharding import PartitionSpec as P

NFFT = 256
BLOCKS = 4
HOP = 128
FREQS = 128
TIME = 640
ROWS = 2 * BLOCKS
GROUP = 32
GROUPS = FREQS // GROUP
AXES = ("space", "tm")
TILE = 256
WIDE = 512
ACROSS = 4
PACKS = (2, 7, 8)
WHOLE = 5
DEPTH = 5
PACK_VMEM = 54 << 20
GRAM_VMEM = 24 << 20
STEPS = ((1, 1), (0, 3), (1, 0), (0, 2), (1, 2), (0, 1), (1, 3), (0, 0))
F32 = jnp.float32
BF16 = jnp.bfloat16


def tables():
    steps = np.arange(NFFT)
    phase = (np.arange(FREQS)[:, None] * steps[None, :] % NFFT) * (2.0 * math.pi / NFFT)
    window = 0.5 - 0.5 * np.cos(steps * (2.0 * math.pi / NFFT))
    full = np.concatenate([window * np.cos(phase), -window * np.sin(phase)], 0)
    full = (full / np.sqrt(np.sum(window * window))).astype(np.float32)
    high = full.astype(ml_dtypes.bfloat16)
    low = (full - high.astype(np.float32)).astype(ml_dtypes.bfloat16)
    split = np.concatenate([high, low], 0)
    sums = (high.astype(np.float64) + low.astype(np.float64)).sum(1, keepdims=True)
    return full, split, sums.astype(np.float32)


def shifted(index, step):
    half, across = index >> 2, index & 3
    return ((half + step[0]) & 1) * ACROSS + ((across + step[1]) & 3)


def parts_of(k):
    return 2 if WHOLE <= k < len(STEPS) - 1 else 1


def pack_kernel(first, end, x_ref, *refs):
    out_refs, (held_ref, sem_ref) = list(refs[:-2]), refs[-2:]
    me = lax.axis_index("tm")
    width = held_ref.shape[3]
    copies = []
    for k in range(first, end):
        lane = pl.multiple_of(shifted(me, STEPS[k]) * width, width)
        copy = pltpu.make_async_copy(
            x_ref.at[:, :, pl.ds(lane, width)], held_ref.at[k - first], sem_ref.at[k - first]
        )
        copy.start()
        copies.append(copy)
    for k in range(first, end):
        copies[k - first].wait()
        size = width // parts_of(k)
        for start in range(0, width, size):
            out_ref = out_refs.pop(0)
            for at in range(0, size, TILE):
                piece = held_ref[k - first, :, :, start + at : start + at + TILE]
                out_ref[:, :, at : at + TILE] = jnp.transpose(piece, (1, 0, 2))


def pack(x, first, end):
    times, count, points = x.shape
    width = points // len(STEPS)
    sizes = [width // parts_of(k) for k in range(first, end) for _ in range(parts_of(k))]
    out = pl.pallas_call(
        functools.partial(pack_kernel, first, end),
        in_specs=[pl.BlockSpec(memory_space=pl.ANY)],
        out_specs=[pl.BlockSpec(memory_space=pltpu.VMEM)] * len(sizes),
        out_shape=[jax.ShapeDtypeStruct((count, times, size), x.dtype) for size in sizes],
        scratch_shapes=[
            pltpu.VMEM((end - first, times, count, width), x.dtype),
            pltpu.SemaphoreType.DMA((end - first,)),
        ],
        compiler_params=pltpu.CompilerParams(
            vmem_limit_bytes=PACK_VMEM if first < len(STEPS) - 1 else GRAM_VMEM
        ),
    )(x)
    out = list(out)
    return [[out.pop(0) for _ in range(parts_of(k))] for k in range(first, end)]


def gram_kernel(start, *refs):
    members = len(STEPS)
    pieces = refs[:members]
    w_ref, split_ref, sums_ref, before_ref = refs[members : members + 4]
    gram_ref, x_ref, mean_ref, coef_ref, acc_ref = refs[members + 4 :]
    me = lax.axis_index("tm")
    count, _, points = x_ref.shape
    steps = pieces[0].shape[1]
    rows = []
    for step in STEPS:
        source = shifted(me, (-step[0], -step[1]))
        rows.append(pl.multiple_of(source * steps, 16))
    acc_ref[...] = jnp.zeros_like(acc_ref)

    for tile in range(points // WIDE):
        here = pl.ds(tile * WIDE, WIDE)
        for k in range(members):
            for v in range(count):
                skip = start if pieces[k].shape[2] > points else 0
                there = pl.ds(skip + tile * WIDE, WIDE)
                x_ref[v, pl.ds(rows[k], steps), here] = pieces[k][v, :, there]
        split = split_ref[...]
        sums = sums_ref[...]
        for v in range(count):
            x = x_ref[v, :, here]
            mean = jnp.sum(x.astype(F32), axis=0, keepdims=True) * (1.0 / TIME)
            mean_ref[v : v + 1, here] = mean
            shift = sums * mean
            for b in range(BLOCKS):
                both = jnp.dot(split, x[b * HOP : b * HOP + NFFT], preferred_element_type=F32)
                coef = (both[:NFFT] + both[NFFT:] - shift).astype(BF16)
                for r in range(2):
                    for g in range(GROUPS):
                        part = coef[r * FREQS + g * GROUP : r * FREQS + (g + 1) * GROUP]
                        c = r * BLOCKS + b
                        coef_ref[g, c * GROUP : (c + 1) * GROUP, v * WIDE : (v + 1) * WIDE] = part
        weights = jnp.concatenate([w_ref[:, pl.ds(start + tile * WIDE, WIDE)]] * count, axis=1)
        for g in range(GROUPS):
            a = coef_ref[g]
            weighted = (a.astype(F32) * weights).astype(BF16)
            acc_ref[g] += lax.dot_general(
                weighted, a, (((1,), (1,)), ((), ())), preferred_element_type=F32
            )

    size = ROWS * GROUP
    row = lax.broadcasted_iota(jnp.int32, (GROUP, size), 0)
    lane = lax.broadcasted_iota(jnp.int32, (GROUP, size), 1)
    same = lane % GROUP == row
    lane1 = lax.broadcasted_iota(jnp.int32, (1, FREQS), 1)
    for g in range(GROUPS):
        last = jnp.zeros((1, FREQS), F32)
        for c in range(ROWS):
            block = acc_ref[g, c * GROUP : (c + 1) * GROUP, :]
            line = jnp.sum(jnp.where(same, block, 0.0), axis=0, keepdims=True)
            if c < BLOCKS:
                mine = lane1 // GROUP == c
                last = last + jnp.where(mine, line[:, FREQS:], 0.0)
            turned = pltpu.roll(line, (size - c * GROUP) % size, 1) if c else line
            at = g * ROWS + c
            gram_ref[at : at + 1, :] = before_ref[at : at + 1, :] + turned[:, :FREQS]
        at = GROUPS * ROWS + g
        gram_ref[at : at + 1, :] = before_ref[at : at + 1, :] + last
    gram_ref[GROUPS * ROWS + GROUPS :, :] = jnp.zeros((ROWS - GROUPS, FREQS), F32)


def gram_terms(pieces, weights, split, sums, before, start, points):
    count = pieces[0].shape[0]
    whole = pl.BlockSpec(memory_space=pltpu.VMEM)
    return pl.pallas_call(
        functools.partial(gram_kernel, start),
        in_specs=[whole] * (len(pieces) + 4),
        out_specs=[whole] * 3,
        out_shape=[
            jax.ShapeDtypeStruct(before.shape, F32),
            jax.ShapeDtypeStruct((count, TIME, points), BF16),
            jax.ShapeDtypeStruct((count, points), F32),
        ],
        scratch_shapes=[
            pltpu.VMEM((GROUPS, ROWS * GROUP, count * WIDE), BF16),
            pltpu.VMEM((GROUPS, ROWS * GROUP, ROWS * GROUP), F32),
        ],
        compiler_params=pltpu.CompilerParams(vmem_limit_bytes=GRAM_VMEM),
        cost_estimate=pl.CostEstimate(
            flops=4 * points * count * (2 * NFFT * NFFT * BLOCKS + ROWS * ROWS * GROUP * FREQS),
            bytes_accessed=4 * count * TIME * points,
            transcendentals=0,
        ),
    )(*pieces, weights.reshape(1, -1), split, sums, before)


def turn(a, by):
    by = by % ROWS
    return a if by == 0 else jnp.concatenate([a[by:], a[:by]], axis=0)


def lanes(a, by):
    by = by % FREQS
    return a if by == 0 else pltpu.roll(a, by, 1)


def full_gram(packed):
    part = lax.broadcasted_iota(jnp.int32, (ROWS, FREQS), 1) // GROUP
    row = lax.broadcasted_iota(jnp.int32, (ROWS, FREQS), 0)
    out = []
    for k in range(BLOCKS):
        total = jnp.zeros((ROWS, FREQS), F32)
        for g in range(GROUPS):
            moved = lanes(packed[g * ROWS : (g + 1) * ROWS], (g - k) * GROUP)
            total = jnp.where(part == g, moved, total)
        out.append(total)
    rest = packed[GROUPS * ROWS :]
    total = jnp.zeros((ROWS, FREQS), F32)
    for delta in range(1 - BLOCKS, BLOCKS):
        moved = lanes(turn(rest, delta), delta * GROUP)
        total = jnp.where((row < BLOCKS) & (part - row == delta), moved, total)
    out.append(total + turn(total, BLOCKS))
    for k in range(BLOCKS + 1, ROWS):
        out.append(turn(out[ROWS - k], k))
    return out


def power_step(spectra, vector):
    return sum(spectra[k] * turn(vector, k) for k in range(ROWS))


def modes_kernel(packed_ref, table_ref, *refs):
    x_refs, mean_refs = refs[:2], refs[2:4]
    modes_ref, spectra_ref, m_ref, sum_ref, out_ref, sem_ref = refs[4:]
    count, _, half = x_refs[0].shape
    gram = full_gram(packed_ref[...])
    trace = jnp.sum(gram[0], axis=0, keepdims=True) + 1e-06
    spectra = [k * (2.0 * BLOCKS / trace) for k in gram]
    row = lax.broadcasted_iota(jnp.int32, (ROWS, FREQS), 0)
    for d in range(ROWS):
        total = jnp.zeros((ROWS, FREQS), F32)
        for c in range(ROWS):
            total = jnp.where(row == c, spectra[(d - c) % ROWS], total)
        spectra_ref[d * ROWS : (d + 1) * ROWS, :] = total
    first = power_step(spectra, jnp.ones((ROWS, FREQS), F32))
    lead = power_step(spectra, first) * (1.0 / math.sqrt(2.0 * BLOCKS))
    padded = jnp.concatenate([lead, jnp.zeros((FREQS - ROWS, FREQS), F32)], axis=0)
    lead = padded.T
    total = [jnp.zeros((FREQS, HOP), F32) for _ in range(BLOCKS + 1)]
    for b in range(BLOCKS):
        for r in range(2):
            c = r * BLOCKS + b
            part = lead[:, c : c + 1] * table_ref[r * FREQS : (r + 1) * FREQS, :]
            total[b] = total[b] + part[:, :HOP]
            total[b + 1] = total[b + 1] + part[:, HOP:]
    total = jnp.concatenate(total, axis=1)
    high = total.astype(BF16)
    low = (total - high.astype(F32)).astype(BF16)
    m_ref[:FREQS] = high
    m_ref[FREQS:] = low
    sum_ref[...] = jnp.sum(high.astype(F32) + low.astype(F32), axis=1, keepdims=True)

    copies = []
    for tile in range(2 * half // WIDE):
        part, at = divmod(tile * WIDE, half)
        out = []
        for v in range(count):
            x = x_refs[part][v, :, at : at + WIDE]
            both = jnp.dot(m_ref[...], x, preferred_element_type=F32)
            shift = sum_ref[...] * mean_refs[part][v : v + 1, at : at + WIDE]
            out.append((both[:FREQS] + both[FREQS:] - shift).astype(BF16))
        out_ref[tile] = pltpu.einshape("vfp->fvp", jnp.stack(out, 0))
        copy = pltpu.make_async_copy(
            out_ref.at[tile], modes_ref.at[:, :, pl.ds(tile * WIDE, WIDE)], sem_ref.at[tile]
        )
        copy.start()
        copies.append(copy)
    for copy in copies:
        copy.wait()


def modes_of(packed, table, series, means):
    count, _, half = series[0].shape
    whole = pl.BlockSpec(memory_space=pltpu.VMEM)
    tiles = 2 * half // WIDE
    return pl.pallas_call(
        modes_kernel,
        in_specs=[whole] * 6,
        out_specs=[pl.BlockSpec(memory_space=pl.ANY), whole],
        out_shape=[
            jax.ShapeDtypeStruct((FREQS, count, 2 * half), BF16),
            jax.ShapeDtypeStruct((ROWS * ROWS, FREQS), F32),
        ],
        scratch_shapes=[
            pltpu.VMEM((2 * FREQS, TIME), BF16),
            pltpu.VMEM((FREQS, 1), F32),
            pltpu.VMEM((tiles, FREQS, count, WIDE), BF16),
            pltpu.SemaphoreType.DMA((tiles,)),
        ],
        compiler_params=pltpu.CompilerParams(vmem_limit_bytes=GRAM_VMEM),
    )(packed, table, *series, *means)


def place(space, tm):
    z, low, core = space // 4, space // 2 % 2, space % 2
    return z, tm // ACROSS * 2 + low, tm % ACROSS, core


def device_at(z, y, x, core):
    return (z * 4 + y % 2 * 2 + core) * 8 + y // 2 * ACROSS + x


def sum_over_devices(value):
    rounds = [[(0, 0, 0, 1)]]
    rounds += [[tuple(k * (a == axis) for a in range(4)) for k in (1, 2, 3)] for axis in (2, 1, 0)]
    for flips in rounds:
        total = value
        for flip in flips:
            pairs = []
            for i in range(128):
                here = place(i // 8, i % 8)
                pairs.append((i, device_at(*(a ^ b for a, b in zip(here, flip)))))
            total = total + lax.ppermute(value, AXES, pairs)
        value = total
    return value


def per_device(members, devices, snapshots, weights):
    table, split, sums = tables()
    split, sums = jnp.asarray(split), jnp.asarray(sums)
    pieces = []
    for first, end in zip((0,) + PACKS[:-1], PACKS):
        pieces += pack(snapshots, first, end)
    sent = []
    for part in range(2):
        for k, step in enumerate(STEPS[:-1]):
            if part < parts_of(k):
                piece = pieces[k][part]
                if len(sent) >= DEPTH:
                    piece = lax.optimization_barrier((piece, sent[-DEPTH]))[0]
                pairs = [(m, shifted(m, step)) for m in range(members)]
                pieces[k][part] = lax.ppermute(piece, "tm", pairs)
                sent.append(pieces[k][part])
    half = weights.shape[0] // 2
    gram = jnp.zeros(((GROUPS + 1) * ROWS, FREQS), F32)
    series, means = [], []
    for part in range(2):
        mine = [piece[part % len(piece)] for piece in pieces]
        gram, x, mean = gram_terms(mine, weights, split, sums, gram, part * half, half)
        series.append(x)
        means.append(mean)
    gram = sum_over_devices(gram)
    modes, spectra = modes_of(gram, jnp.asarray(table), series, means)
    spectra = spectra.T.reshape(FREQS, ROWS, ROWS)
    return (modes, spectra)


def solution(mesh):
    members = mesh.shape["tm"]
    devices = members * mesh.shape["space"]
    in_specs = (P("tm", None, "space"), P(AXES))
    out_specs = (P(None, None, AXES), P())
    return jax.shard_map(
        functools.partial(per_device, members, devices),
        mesh=mesh,
        in_specs=in_specs,
        out_specs=out_specs,
        check_vma=False,
    )
```

```python
import functools
import math

import jax
import jax.numpy as jnp
import ml_dtypes
import numpy as np
from jax import lax
from jax.experimental import pallas as pl
from jax.experimental.pallas import tpu as pltpu
from jax.sharding import PartitionSpec as P

NFFT = 256
BLOCKS = 4
HOP = 128
FREQS = 128
TIME = 640
ROWS = 2 * BLOCKS
GROUP = 32
GROUPS = FREQS // GROUP
AXES = ("space", "tm")
TILE = 256
WIDE = 512
ACROSS = 4
PACKS = (2, 4, 7, 8)
WHOLE = 5
DEPTH = 5
PACK_VMEM = 54 << 20
GRAM_VMEM = 24 << 20
STEPS = ((1, 1), (0, 3), (1, 0), (0, 2), (1, 2), (0, 1), (1, 3), (0, 0))
F32 = jnp.float32
BF16 = jnp.bfloat16


def tables():
    steps = np.arange(NFFT)
    phase = (np.arange(FREQS)[:, None] * steps[None, :] % NFFT) * (2.0 * math.pi / NFFT)
    window = 0.5 - 0.5 * np.cos(steps * (2.0 * math.pi / NFFT))
    full = np.concatenate([window * np.cos(phase), -window * np.sin(phase)], 0)
    full = (full / np.sqrt(np.sum(window * window))).astype(np.float32)
    high = full.astype(ml_dtypes.bfloat16)
    low = (full - high.astype(np.float32)).astype(ml_dtypes.bfloat16)
    split = np.concatenate([high, low], 0)
    sums = (high.astype(np.float64) + low.astype(np.float64)).sum(1, keepdims=True)
    return full, split, sums.astype(np.float32)


def shifted(index, step):
    half, across = index >> 2, index & 3
    return ((half + step[0]) & 1) * ACROSS + ((across + step[1]) & 3)


def parts_of(k):
    return 2 if WHOLE <= k < len(STEPS) - 1 else 1


def pack_kernel(first, end, x_ref, *refs):
    out_refs, (held_ref, sem_ref) = list(refs[:-2]), refs[-2:]
    me = lax.axis_index("tm")
    width = held_ref.shape[3]
    copies = []
    for k in range(first, end):
        lane = pl.multiple_of(shifted(me, STEPS[k]) * width, width)
        copy = pltpu.make_async_copy(
            x_ref.at[:, :, pl.ds(lane, width)], held_ref.at[k - first], sem_ref.at[k - first]
        )
        copy.start()
        copies.append(copy)
    for k in range(first, end):
        copies[k - first].wait()
        size = width // parts_of(k)
        for start in range(0, width, size):
            out_ref = out_refs.pop(0)
            for at in range(0, size, TILE):
                piece = held_ref[k - first, :, :, start + at : start + at + TILE]
                out_ref[:, :, at : at + TILE] = jnp.transpose(piece, (1, 0, 2))


def pack(x, first, end):
    times, count, points = x.shape
    width = points // len(STEPS)
    sizes = [width // parts_of(k) for k in range(first, end) for _ in range(parts_of(k))]
    out = pl.pallas_call(
        functools.partial(pack_kernel, first, end),
        in_specs=[pl.BlockSpec(memory_space=pl.ANY)],
        out_specs=[pl.BlockSpec(memory_space=pltpu.VMEM)] * len(sizes),
        out_shape=[jax.ShapeDtypeStruct((count, times, size), x.dtype) for size in sizes],
        scratch_shapes=[
            pltpu.VMEM((end - first, times, count, width), x.dtype),
            pltpu.SemaphoreType.DMA((end - first,)),
        ],
        compiler_params=pltpu.CompilerParams(
            vmem_limit_bytes=PACK_VMEM if first < len(STEPS) - 1 else GRAM_VMEM
        ),
    )(x)
    out = list(out)
    return [[out.pop(0) for _ in range(parts_of(k))] for k in range(first, end)]


def gram_kernel(start, *refs):
    members = len(STEPS)
    pieces = refs[:members]
    w_ref, split_ref, sums_ref, before_ref = refs[members : members + 4]
    gram_ref, x_ref, mean_ref, coef_ref, acc_ref = refs[members + 4 :]
    me = lax.axis_index("tm")
    count, _, points = x_ref.shape
    steps = pieces[0].shape[1]
    rows = []
    for step in STEPS:
        source = shifted(me, (-step[0], -step[1]))
        rows.append(pl.multiple_of(source * steps, 16))
    acc_ref[...] = jnp.zeros_like(acc_ref)

    for tile in range(points // WIDE):
        here = pl.ds(tile * WIDE, WIDE)
        for k in range(members):
            for v in range(count):
                skip = start if pieces[k].shape[2] > points else 0
                there = pl.ds(skip + tile * WIDE, WIDE)
                x_ref[v, pl.ds(rows[k], steps), here] = pieces[k][v, :, there]
        split = split_ref[...]
        sums = sums_ref[...]
        for v in range(count):
            x = x_ref[v, :, here]
            mean = jnp.sum(x.astype(F32), axis=0, keepdims=True) * (1.0 / TIME)
            mean_ref[v : v + 1, here] = mean
            shift = sums * mean
            for b in range(BLOCKS):
                both = jnp.dot(split, x[b * HOP : b * HOP + NFFT], preferred_element_type=F32)
                coef = (both[:NFFT] + both[NFFT:] - shift).astype(BF16)
                for r in range(2):
                    for g in range(GROUPS):
                        part = coef[r * FREQS + g * GROUP : r * FREQS + (g + 1) * GROUP]
                        c = r * BLOCKS + b
                        coef_ref[g, c * GROUP : (c + 1) * GROUP, v * WIDE : (v + 1) * WIDE] = part
        weights = jnp.concatenate([w_ref[:, pl.ds(start + tile * WIDE, WIDE)]] * count, axis=1)
        for g in range(GROUPS):
            a = coef_ref[g]
            weighted = (a.astype(F32) * weights).astype(BF16)
            acc_ref[g] += lax.dot_general(
                weighted, a, (((1,), (1,)), ((), ())), preferred_element_type=F32
            )

    size = ROWS * GROUP
    row = lax.broadcasted_iota(jnp.int32, (GROUP, size), 0)
    lane = lax.broadcasted_iota(jnp.int32, (GROUP, size), 1)
    same = lane % GROUP == row
    lane1 = lax.broadcasted_iota(jnp.int32, (1, FREQS), 1)
    for g in range(GROUPS):
        last = jnp.zeros((1, FREQS), F32)
        for c in range(ROWS):
            block = acc_ref[g, c * GROUP : (c + 1) * GROUP, :]
            line = jnp.sum(jnp.where(same, block, 0.0), axis=0, keepdims=True)
            if c < BLOCKS:
                mine = lane1 // GROUP == c
                last = last + jnp.where(mine, line[:, FREQS:], 0.0)
            turned = pltpu.roll(line, (size - c * GROUP) % size, 1) if c else line
            at = g * ROWS + c
            gram_ref[at : at + 1, :] = before_ref[at : at + 1, :] + turned[:, :FREQS]
        at = GROUPS * ROWS + g
        gram_ref[at : at + 1, :] = before_ref[at : at + 1, :] + last
    gram_ref[GROUPS * ROWS + GROUPS :, :] = jnp.zeros((ROWS - GROUPS, FREQS), F32)


def gram_terms(pieces, weights, split, sums, before, start, points):
    count = pieces[0].shape[0]
    whole = pl.BlockSpec(memory_space=pltpu.VMEM)
    return pl.pallas_call(
        functools.partial(gram_kernel, start),
        in_specs=[whole] * (len(pieces) + 4),
        out_specs=[whole] * 3,
        out_shape=[
            jax.ShapeDtypeStruct(before.shape, F32),
            jax.ShapeDtypeStruct((count, TIME, points), BF16),
            jax.ShapeDtypeStruct((count, points), F32),
        ],
        scratch_shapes=[
            pltpu.VMEM((GROUPS, ROWS * GROUP, count * WIDE), BF16),
            pltpu.VMEM((GROUPS, ROWS * GROUP, ROWS * GROUP), F32),
        ],
        compiler_params=pltpu.CompilerParams(vmem_limit_bytes=GRAM_VMEM),
        cost_estimate=pl.CostEstimate(
            flops=4 * points * count * (2 * NFFT * NFFT * BLOCKS + ROWS * ROWS * GROUP * FREQS),
            bytes_accessed=4 * count * TIME * points,
            transcendentals=0,
        ),
    )(*pieces, weights.reshape(1, -1), split, sums, before)


def turn(a, by):
    by = by % ROWS
    return a if by == 0 else jnp.concatenate([a[by:], a[:by]], axis=0)


def lanes(a, by):
    by = by % FREQS
    return a if by == 0 else pltpu.roll(a, by, 1)


def full_gram(packed):
    part = lax.broadcasted_iota(jnp.int32, (ROWS, FREQS), 1) // GROUP
    row = lax.broadcasted_iota(jnp.int32, (ROWS, FREQS), 0)
    out = []
    for k in range(BLOCKS):
        total = jnp.zeros((ROWS, FREQS), F32)
        for g in range(GROUPS):
            moved = lanes(packed[g * ROWS : (g + 1) * ROWS], (g - k) * GROUP)
            total = jnp.where(part == g, moved, total)
        out.append(total)
    rest = packed[GROUPS * ROWS :]
    total = jnp.zeros((ROWS, FREQS), F32)
    for delta in range(1 - BLOCKS, BLOCKS):
        moved = lanes(turn(rest, delta), delta * GROUP)
        total = jnp.where((row < BLOCKS) & (part - row == delta), moved, total)
    out.append(total + turn(total, BLOCKS))
    for k in range(BLOCKS + 1, ROWS):
        out.append(turn(out[ROWS - k], k))
    return out


def power_step(spectra, vector):
    return sum(spectra[k] * turn(vector, k) for k in range(ROWS))


def modes_kernel(packed_ref, table_ref, *refs):
    x_refs, mean_refs = refs[:2], refs[2:4]
    modes_ref, spectra_ref, m_ref, sum_ref, out_ref, sem_ref = refs[4:]
    count, _, half = x_refs[0].shape
    gram = full_gram(packed_ref[...])
    trace = jnp.sum(gram[0], axis=0, keepdims=True) + 1e-06
    spectra = [k * (2.0 * BLOCKS / trace) for k in gram]
    row = lax.broadcasted_iota(jnp.int32, (ROWS, FREQS), 0)
    for d in range(ROWS):
        total = jnp.zeros((ROWS, FREQS), F32)
        for c in range(ROWS):
            total = jnp.where(row == c, spectra[(d - c) % ROWS], total)
        spectra_ref[d * ROWS : (d + 1) * ROWS, :] = total
    first = power_step(spectra, jnp.ones((ROWS, FREQS), F32))
    lead = power_step(spectra, first) * (1.0 / math.sqrt(2.0 * BLOCKS))
    padded = jnp.concatenate([lead, jnp.zeros((FREQS - ROWS, FREQS), F32)], axis=0)
    lead = padded.T
    total = [jnp.zeros((FREQS, HOP), F32) for _ in range(BLOCKS + 1)]
    for b in range(BLOCKS):
        for r in range(2):
            c = r * BLOCKS + b
            part = lead[:, c : c + 1] * table_ref[r * FREQS : (r + 1) * FREQS, :]
            total[b] = total[b] + part[:, :HOP]
            total[b + 1] = total[b + 1] + part[:, HOP:]
    total = jnp.concatenate(total, axis=1)
    high = total.astype(BF16)
    low = (total - high.astype(F32)).astype(BF16)
    m_ref[:FREQS] = high
    m_ref[FREQS:] = low
    sum_ref[...] = jnp.sum(high.astype(F32) + low.astype(F32), axis=1, keepdims=True)

    copies = []
    for tile in range(2 * half // WIDE):
        part, at = divmod(tile * WIDE, half)
        out = []
        for v in range(count):
            x = x_refs[part][v, :, at : at + WIDE]
            both = jnp.dot(m_ref[...], x, preferred_element_type=F32)
            shift = sum_ref[...] * mean_refs[part][v : v + 1, at : at + WIDE]
            out.append((both[:FREQS] + both[FREQS:] - shift).astype(BF16))
        out_ref[tile] = pltpu.einshape("vfp->fvp", jnp.stack(out, 0))
        copy = pltpu.make_async_copy(
            out_ref.at[tile], modes_ref.at[:, :, pl.ds(tile * WIDE, WIDE)], sem_ref.at[tile]
        )
        copy.start()
        copies.append(copy)
    for copy in copies:
        copy.wait()


def modes_of(packed, table, series, means):
    count, _, half = series[0].shape
    whole = pl.BlockSpec(memory_space=pltpu.VMEM)
    tiles = 2 * half // WIDE
    return pl.pallas_call(
        modes_kernel,
        in_specs=[whole] * 6,
        out_specs=[pl.BlockSpec(memory_space=pl.ANY), whole],
        out_shape=[
            jax.ShapeDtypeStruct((FREQS, count, 2 * half), BF16),
            jax.ShapeDtypeStruct((ROWS * ROWS, FREQS), F32),
        ],
        scratch_shapes=[
            pltpu.VMEM((2 * FREQS, TIME), BF16),
            pltpu.VMEM((FREQS, 1), F32),
            pltpu.VMEM((tiles, FREQS, count, WIDE), BF16),
            pltpu.SemaphoreType.DMA((tiles,)),
        ],
        compiler_params=pltpu.CompilerParams(vmem_limit_bytes=GRAM_VMEM),
    )(packed, table, *series, *means)


def place(space, tm):
    z, low, core = space // 4, space // 2 % 2, space % 2
    return z, tm // ACROSS * 2 + low, tm % ACROSS, core


def device_at(z, y, x, core):
    return (z * 4 + y % 2 * 2 + core) * 8 + y // 2 * ACROSS + x


def sum_over_devices(value):
    rounds = [[(0, 0, 0, 1)]]
    rounds += [[tuple(k * (a == axis) for a in range(4)) for k in (1, 2, 3)] for axis in (2, 1, 0)]
    for flips in rounds:
        total = value
        for flip in flips:
            pairs = []
            for i in range(128):
                here = place(i // 8, i % 8)
                pairs.append((i, device_at(*(a ^ b for a, b in zip(here, flip)))))
            total = total + lax.ppermute(value, AXES, pairs)
        value = total
    return value


def per_device(members, devices, snapshots, weights):
    table, split, sums = tables()
    split, sums = jnp.asarray(split), jnp.asarray(sums)
    pieces = []
    for first, end in zip((0,) + PACKS[:-1], PACKS):
        pieces += pack(snapshots, first, end)
    sent = []
    for part in range(2):
        for k, step in enumerate(STEPS[:-1]):
            if part < parts_of(k):
                piece = pieces[k][part]
                if len(sent) >= DEPTH:
                    piece = lax.optimization_barrier((piece, sent[-DEPTH]))[0]
                pairs = [(m, shifted(m, step)) for m in range(members)]
                pieces[k][part] = lax.ppermute(piece, "tm", pairs)
                sent.append(pieces[k][part])
    half = weights.shape[0] // 2
    gram = jnp.zeros(((GROUPS + 1) * ROWS, FREQS), F32)
    series, means = [], []
    for part in range(2):
        mine = [piece[part % len(piece)] for piece in pieces]
        gram, x, mean = gram_terms(mine, weights, split, sums, gram, part * half, half)
        series.append(x)
        means.append(mean)
    gram = sum_over_devices(gram)
    modes, spectra = modes_of(gram, jnp.asarray(table), series, means)
    spectra = spectra.T.reshape(FREQS, ROWS, ROWS)
    return (modes, spectra)


def solution(mesh):
    members = mesh.shape["tm"]
    devices = members * mesh.shape["space"]
    in_specs = (P("tm", None, "space"), P(AXES))
    out_specs = (P(None, None, AXES), P())
    return jax.shard_map(
        functools.partial(per_device, members, devices),
        mesh=mesh,
        in_specs=in_specs,
        out_specs=out_specs,
        check_vma=False,
    )
```
